1024 devices in a mesh: blk: 32 (over z_hi, y), col: 32 (over x, z_lo, core).
Axes of the slice: x: 8, y: 8, z: 8 (z_hi: 4, z_lo: 2; z = z_hi * 2 + z_lo), core: 2. Of those that a mesh axis runs over, the one named last changes fastest.
Arguments:
- pvals: bfloat16 [256, 4, 128, 128], P('blk'), may hold values from -1 to 1
- pcols: int32 [256, 4], P('blk'), may hold values from 0 to 255, as said below
- out_cols: int32 [256, 32], P('blk', 'col'), may hold values from 0 to 255, as said below
Outputs:
- purified: bfloat16 [256, 32, 128, 128], P('blk', 'col')
The draws below stay inside these ranges and needn't reach their ends.
Inputs may be any that keep to these rules, and one draw needn't show every extreme that they name: `pcols`: each row r lists 4 distinct block columns, each within 8 of r counted cyclically modulo 256; slot 0 is r itself. `out_cols`: each row r lists 32 distinct block columns, each within 16 of r counted cyclically modulo 256.
All inputs are finite; a program needn't handle non-finite values.
Results may differ from the reference program's by a relative error of at most 0.0049.
Values may be sent and summed in bfloat16 or wider, within the bound.
No kernel may reach another device: no remote copies, remote signals or barrier semaphores. Data moves between devices by JAX's collectives and lax.ppermute only.
A program may use at most 64 MiB of HBM per device.

```python
import jax
import jax.numpy as jnp
from jax import lax

BS = 128
K = 4
NB = 256
KOT = 32
HR = 8
OW = 16


def banded_offsets(key, half_width, count):
    row_keys = jax.random.split(key, NB)
    candidates = jnp.arange(-half_width, half_width + 1).astype(jnp.int32)

    def shuffle_row(row_key):
        return jax.random.permutation(row_key, 2 * half_width + 1)
    shuffled = jax.vmap(shuffle_row)(row_keys)
    return candidates[shuffled[:, :count]]


def draw_pcols(key, part):
    key = jax.random.fold_in(key, 11)
    row_keys = jax.random.split(key, NB)
    candidates = jnp.concatenate([jnp.arange(-HR, 0), jnp.arange(1, HR + 1)]).astype(jnp.int32)

    def shuffle_row(row_key):
        return jax.random.permutation(row_key, 2 * HR)
    shuffled = jax.vmap(shuffle_row)(row_keys)
    offsets = jnp.concatenate([jnp.zeros((NB, 1), jnp.int32), candidates[shuffled[:, :K - 1]]], 1)
    row_ids = jnp.arange(NB, dtype=jnp.int32)[:, None]
    return jnp.mod(row_ids + offsets, NB).astype(jnp.int32)


def draw_out_cols(key, part):
    key = jax.random.fold_in(key, 23)
    offsets = banded_offsets(key, OW, KOT)
    row_ids = jnp.arange(NB, dtype=jnp.int32)[:, None]
    return jnp.mod(row_ids + offsets, NB).astype(jnp.int32)


def block_scale(key, shape, pieces, least, top_value):
    def one(axis_at, shards_of):
        heights = jax.random.uniform(jax.random.fold_in(jax.random.fold_in(key, 6), axis_at), (shards_of,), jnp.float32, least / len(pieces), top_value / len(pieces))
        return jnp.repeat(jnp.exp(heights), shape[axis_at] // shards_of).reshape((-1,) + (1,) * (len(shape) - axis_at - 1))

    factor_of = one(*pieces[0])
    for cut in pieces[1:]:
        factor_of = factor_of * one(*cut)
    return factor_of


def scatter_about(stream_key, shape, spread, bound, pieces=(), kind=jnp.bfloat16):
    array = spread * jax.random.normal(stream_key, shape, jnp.float32)
    if pieces:
        array = array * block_scale(stream_key, shape, pieces, -0.22, 0.18)
    return jnp.clip(array, -bound, bound).astype(kind)


def setup_inputs(seed: int = 0) -> dict:
    key_of = jax.random.split(jax.random.key(seed), 4)
    pvals = scatter_about(key_of[0], (NB, K, BS, BS), (BS // 4) ** -0.5, 1.0, ((0, 32),))
    pcols = draw_pcols(jax.random.fold_in(key_of[3], 71), 0)
    out_cols = draw_out_cols(jax.random.fold_in(key_of[3], 71), 0)
    return {"pvals": pvals, "pcols": pcols, "out_cols": out_cols}


def reference(pvals, pcols, out_cols):
    def square_row(inputs):
        row_blocks, row_columns, row_wanted = inputs
        fetched = pvals[row_columns]
        fetched_columns = pcols[row_columns]
        matches = (fetched_columns[None, :, :] == row_wanted[:, None, None]).astype(jnp.float32)
        chosen = jnp.einsum("sab,abij->saij", matches, fetched.astype(jnp.float32)).astype(jnp.bfloat16)
        product = jnp.einsum("aij,sajk->sik", row_blocks.astype(jnp.float32), chosen.astype(jnp.float32))
        return product.astype(jnp.bfloat16)

    squared = lax.map(square_row, (pvals, pcols, out_cols))

    def cube_row(inputs):
        squared_row, row_wanted = inputs
        fetched = pvals[row_wanted]
        fetched_columns = pcols[row_wanted]
        matches = (fetched_columns[None, :, :] == row_wanted[:, None, None]).astype(jnp.float32)
        chosen = jnp.einsum("oqb,qbij->oqij", matches, fetched.astype(jnp.float32)).astype(jnp.bfloat16)
        return jnp.einsum("qij,oqjk->oik", squared_row.astype(jnp.float32), chosen.astype(jnp.float32))

    cubed = lax.map(cube_row, (squared, out_cols))
    return (3.0 * squared.astype(jnp.float32) - 2.0 * cubed).astype(jnp.bfloat16)
```

```python
import jax
import jax.numpy as jnp
from jax import lax
from jax.experimental import pallas as pl
from jax.experimental.pallas import tpu as pltpu
from jax.sharding import PartitionSpec as P

REACH = 2
SHIFTS = (1, -1, 2, -2)


def from_blk(array, distance):
    n = lax.axis_size("blk")
    return lax.ppermute(array, "blk", [((i + distance) % n, i) for i in range(n)])


def from_col(array, source_of):
    n = lax.axis_size("col")
    return lax.ppermute(array, "col", [(source_of(i), i) for i in range(n)])


def purify_kernel(
    layout, bs, slots, sites_ref, cols_ref, wanted_ref, skipped_ref, *refs
):
    pieces, out_ref, window, picks, sems = refs[:-4], refs[-4], refs[-3], refs[-2], refs[-1]
    row_count = out_ref.shape[0]
    nothing = window.shape[0] // bs - 1
    copies = []
    for ref, moves in zip(pieces, layout, strict=True):
        for source, target, site, rows in moves:
            start = pl.multiple_of(target + sites_ref[site], bs)
            copies.append(
                pltpu.make_async_copy(
                    ref.at[pl.ds(source, rows)],
                    window.at[pl.ds(start, rows)],
                    sems.at[len(copies)],
                )
            )
            copies[-1].start()
    window[pl.ds(nothing * bs, bs)] = jnp.zeros((bs, window.shape[1]), window.dtype)

    first = REACH * row_count

    def find_row(r, carry):
        column, skipped = wanted_ref[r], skipped_ref[r]
        for a in range(slots):
            base = cols_ref[(first + r) * slots + a] * slots
            for b in range(slots):
                q = cols_ref[base + b]
                found = jnp.int32(nothing)
                for m in range(slots):
                    found = jnp.where(cols_ref[q * slots + m] == column, q * slots + m, found)
                found = jnp.where(q == skipped, nothing, found)
                picks[r * 32 + a * slots + b] = found
                picks[r * 32 + 16 + a * slots + b] = jnp.where(q == column, base + b, nothing)
        return carry

    lax.fori_loop(0, row_count, find_row, 0)
    for copy in copies:
        copy.wait()

    def block(index):
        return window[pl.ds(pl.multiple_of(index * bs, bs), bs)]

    def stack(indices, axis):
        return jnp.concatenate([block(i) for i in indices], axis=axis)

    for r in range(row_count):
        direct, high, low = [], [], []
        for a in range(slots):
            base = cols_ref[(first + r) * slots + a] * slots
            left = stack([base + b for b in range(slots)], 1)
            right = stack([picks[r * 32 + a * slots + b] for b in range(slots)], 0)
            total = jnp.dot(left, right, preferred_element_type=jnp.float32)
            top = total.astype(jnp.bfloat16)
            high.append(top)
            low.append((total - top.astype(jnp.float32)).astype(jnp.bfloat16))
            one = [block(picks[r * 32 + 16 + a * slots + b]) for b in range(slots)]
            direct.append((one[0] + one[1]) + (one[2] + one[3]))
        left = stack([(first + r) * slots + a for a in range(slots)], 1)
        right = jnp.concatenate(
            [jnp.concatenate(part, 0) for part in (direct, high, low)], 1
        )
        sums = jnp.dot(left, right, preferred_element_type=jnp.float32)
        squared = sums[:, :bs].astype(jnp.bfloat16).astype(jnp.float32)
        cubed = sums[:, bs : 2 * bs] + sums[:, 2 * bs :]
        out_ref[r, 0] = (3.0 * squared - 2.0 * cubed).astype(jnp.bfloat16)


def body(pvals, pcols, out_cols):
    row_count, slots, bs, _ = pvals.shape
    panel = row_count * slots * bs
    quarter, eighth = panel // 4, panel // 8
    total_rows = row_count * lax.axis_size("blk")
    own = lax.axis_index("blk")
    place = lax.axis_index("col")
    window_start = (own - REACH) * row_count

    parity, core = (place // 4) % 2, place % 2
    mine = 2 * parity + core
    flat = pvals.reshape(panel, bs)
    own_cols = pcols.reshape(-1)
    tail = jnp.zeros((16, bs), jnp.bfloat16)
    tail = tail.at[0, : own_cols.shape[0]].set(own_cols.astype(jnp.bfloat16))
    parcel = jnp.concatenate(
        [lax.dynamic_slice_in_dim(flat, mine * quarter, quarter, 0), tail], 0
    )
    arrived = [from_blk(parcel, d) for d in SHIFTS]
    from_left = from_col(
        jnp.concatenate([x[:eighth] for x in arrived], 0), lambda i: (i - 4) % 32
    )
    from_right = from_col(
        jnp.concatenate([x[eighth:quarter] for x in arrived], 0), lambda i: (i + 4) % 32
    )
    other = from_col(jnp.concatenate(arrived, 0), lambda i: i ^ 1)
    other_left = from_col(from_left, lambda i: i ^ 1)
    other_right = from_col(from_right, lambda i: i ^ 1)

    def local(ids):
        return jnp.mod(ids - window_start, total_rows).astype(jnp.int32)

    by_shift = {d: x[quarter, : own_cols.shape[0]] for d, x in zip(SHIFTS, arrived)}
    by_shift[0] = own_cols.astype(jnp.bfloat16)
    window_cols = jnp.concatenate([by_shift[d] for d in range(-REACH, REACH + 1)])
    window_cols = local(window_cols.astype(jnp.int32))
    wanted = local(out_cols[:, 0])
    bound = REACH * row_count
    offsets = jnp.mod(wanted - jnp.arange(row_count), total_rows)
    missing = bound * (2 * bound + 1) - lax.psum(offsets, "col")
    skipped = missing + jnp.arange(row_count, dtype=jnp.int32)

    sites = jnp.stack([2 * parity + core, 2 * (1 - parity) + core, 2 * parity + 1 - core, 2 * (1 - parity) + 1 - core])
    sites = jnp.concatenate([sites * quarter, jnp.zeros((1,), jnp.int32)]).astype(jnp.int32)
    pieces = [flat, *arrived, from_left, from_right, other, other_left, other_right]
    at = [(d + REACH) * panel for d in SHIFTS]
    layout = [[(0, REACH * panel, 4, panel)]]
    layout += [[(0, t, 0, quarter)] for t in at]
    layout += [[(j * eighth, t, 1, eighth) for j, t in enumerate(at)]]
    layout += [[(j * eighth, t + eighth, 1, eighth) for j, t in enumerate(at)]]
    layout += [[(j * (quarter + 16), t, 2, quarter) for j, t in enumerate(at)]]
    layout += [[(j * eighth, t, 3, eighth) for j, t in enumerate(at)]]
    layout += [[(j * eighth, t + eighth, 3, eighth) for j, t in enumerate(at)]]
    return call_kernel(layout, bs, slots, row_count, sites, window_cols, wanted, skipped, pieces)


def call_kernel(layout, bs, slots, row_count, sites, window_cols, wanted, skipped, pieces):
    window_rows = (2 * REACH + 1) * row_count * slots * bs
    smem = pl.BlockSpec(memory_space=pltpu.SMEM)
    return pl.pallas_call(
        lambda *refs: purify_kernel(layout, bs, slots, *refs),
        out_shape=jax.ShapeDtypeStruct((row_count, 1, bs, bs), jnp.bfloat16),
        in_specs=[smem] * 4 + [pl.BlockSpec(memory_space=pl.ANY)] * len(pieces),
        out_specs=pl.BlockSpec(memory_space=pltpu.VMEM),
        scratch_shapes=[
            pltpu.VMEM((window_rows + bs, bs), jnp.bfloat16),
            pltpu.SMEM((row_count * 32,), jnp.int32),
            pltpu.SemaphoreType.DMA((sum(map(len, layout)),)),
        ],
        compiler_params=pltpu.CompilerParams(vmem_limit_bytes=24 * 2**20),
        name="purify",
    )(sites, window_cols, wanted, skipped, *pieces)


def solution(mesh):
    placed = (P("blk", None, None, None), P("blk", None), P("blk", "col"))
    return jax.shard_map(
        body, mesh=mesh, in_specs=placed, out_specs=P("blk", "col", None, None), check_vma=False
    )
```

```python
import jax
import jax.numpy as jnp
from jax import lax
from jax.experimental import pallas as pl
from jax.experimental.pallas import tpu as pltpu
from jax.sharding import PartitionSpec as P

REACH = 2
def swap_routes(partner_of):
    return [(partner_of(i), i) for i in range(lax.axis_size("blk"))]


def col_routes(source_of):
    return [(source_of(i) % lax.axis_size("col"), i) for i in range(lax.axis_size("col"))]


def purify_kernel(layout, bs, slots, targets_ref, cols_ref, wanted_ref, skipped_ref, *refs):
    pieces, out_ref, window, picks, sems = refs[:-4], refs[-4], refs[-3], refs[-2], refs[-1]
    row_count = out_ref.shape[0]
    nothing = window.shape[0] // bs - 1
    copies = []
    for ref, moves in zip(pieces, layout, strict=True):
        for source, rows in moves:
            start = pl.multiple_of(targets_ref[len(copies)], bs)
            copies.append(
                pltpu.make_async_copy(
                    ref.at[pl.ds(source, rows)],
                    window.at[pl.ds(start, rows)],
                    sems.at[len(copies)],
                )
            )
            copies[-1].start()
    window[pl.ds(nothing * bs, bs)] = jnp.zeros((bs, window.shape[1]), window.dtype)

    first = REACH * row_count

    def find_row(r, carry):
        column, skipped = wanted_ref[r], skipped_ref[r]
        for a in range(slots):
            base = cols_ref[(first + r) * slots + a] * slots
            for b in range(slots):
                q = cols_ref[base + b]
                found = jnp.int32(nothing)
                for m in range(slots):
                    found = jnp.where(cols_ref[q * slots + m] == column, q * slots + m, found)
                found = jnp.where(q == skipped, nothing, found)
                picks[r * 32 + a * slots + b] = found
                picks[r * 32 + 16 + a * slots + b] = jnp.where(q == column, base + b, nothing)
        return carry

    lax.fori_loop(0, row_count, find_row, 0)
    for copy in copies:
        copy.wait()

    def block(index):
        return window[pl.ds(pl.multiple_of(index * bs, bs), bs)]

    def stack(indices, axis):
        return jnp.concatenate([block(i) for i in indices], axis=axis)

    for r in range(row_count):
        direct, high, low = [], [], []
        for a in range(slots):
            base = cols_ref[(first + r) * slots + a] * slots
            left = stack([base + b for b in range(slots)], 1)
            right = stack([picks[r * 32 + a * slots + b] for b in range(slots)], 0)
            total = jnp.dot(left, right, preferred_element_type=jnp.float32)
            top = total.astype(jnp.bfloat16)
            high.append(top)
            low.append((total - top.astype(jnp.float32)).astype(jnp.bfloat16))
            one = [block(picks[r * 32 + 16 + a * slots + b]) for b in range(slots)]
            direct.append((one[0] + one[1]) + (one[2] + one[3]))
        left = stack([(first + r) * slots + a for a in range(slots)], 1)
        right = jnp.concatenate(
            [jnp.concatenate(part, 0) for part in (direct, high, low)], 1
        )
        sums = jnp.dot(left, right, preferred_element_type=jnp.float32)
        squared = sums[:, :bs].astype(jnp.bfloat16).astype(jnp.float32)
        cubed = sums[:, bs : 2 * bs] + sums[:, 2 * bs :]
        out_ref[r, 0] = (3.0 * squared - 2.0 * cubed).astype(jnp.bfloat16)


def body(pvals, pcols, out_cols):
    row_count, slots, bs, _ = pvals.shape
    panel = row_count * slots * bs
    quarter, eighth = panel // 4, panel // 8
    total_rows = row_count * lax.axis_size("blk")
    own = lax.axis_index("blk")
    place = lax.axis_index("col")
    window_start = (own - REACH) * row_count
    parity, core = jnp.bitwise_and(place >> 2, 1), jnp.bitwise_and(place, 1)
    flat = pvals.reshape(panel, bs)
    own_cols = pcols.reshape(-1)
    tail = jnp.zeros((16, bs), jnp.bfloat16)
    tail = tail.at[0, : own_cols.shape[0]].set(own_cols.astype(jnp.bfloat16))
    mine = lax.dynamic_slice_in_dim(flat, (2 * parity + core) * quarter, quarter, 0)
    parcel = jnp.concatenate([mine, tail], 0)

    count = lax.axis_size("blk")
    late = [
        lax.ppermute(parcel, "blk", swap_routes(lambda i, d=d: (((i + d) ^ d) - d) % count))
        for d in (1, 2)
    ]
    early = [lax.ppermute(parcel, "blk", swap_routes(lambda i, d=d: i ^ d)) for d in (1, 2)]

    def spread(arrived):
        left = lax.ppermute(
            jnp.concatenate([x[:eighth] for x in arrived], 0), "col", col_routes(lambda i: i - 4)
        )
        right = lax.ppermute(
            jnp.concatenate([x[eighth:quarter] for x in arrived], 0), "col", col_routes(lambda i: i + 4)
        )
        other = lax.ppermute(jnp.concatenate(arrived, 0), "col", col_routes(lambda i: i ^ 1))
        sides = lax.ppermute(jnp.concatenate([left, right], 0), "col", col_routes(lambda i: i ^ 1))
        return [*arrived, left, right, other, sides]

    def local(ids):
        return jnp.bitwise_and(ids - window_start, total_rows - 1).astype(jnp.int32)

    def listed(x):
        return x[quarter, : own_cols.shape[0]]

    odd = [jnp.bitwise_and(own, d) != 0 for d in (1, 2)]
    ahead = [jnp.where(o, listed(x), listed(y)) for o, x, y in zip(odd, late, early)]
    behind = [jnp.where(o, listed(y), listed(x)) for o, x, y in zip(odd, late, early)]
    window_cols = jnp.concatenate(
        [behind[1], behind[0], own_cols.astype(jnp.bfloat16), ahead[0], ahead[1]]
    )
    window_cols = local(window_cols.astype(jnp.int32))
    wanted = local(out_cols[:, 0])
    bound = REACH * row_count
    rows = jnp.arange(row_count, dtype=jnp.int32)
    offsets = jnp.bitwise_and(wanted - rows, total_rows - 1)
    skipped = bound * (2 * bound + 1) - lax.psum(offsets, "col") + rows

    early_pieces = spread(early)
    late, early_pieces[2:4] = lax.optimization_barrier((late, early_pieces[2:4]))
    pieces = [flat] + early_pieces + spread(late)
    site = {
        (h, c): (2 * (parity ^ h) + (core ^ c)) * quarter for h in (0, 1) for c in (0, 1)
    }
    layout, targets = [[(0, panel)]], [jnp.int32(REACH * panel)]
    for way in (1, -1):
        tops = [(REACH + jnp.where(o, -way, way) * d) * panel for o, d in zip(odd, (1, 2))]
        for top in tops:
            layout.append([(0, quarter)])
            targets.append(top + site[0, 0])
        for shift in (0, eighth):
            layout.append([(0, eighth), (eighth, eighth)])
            targets += [top + site[1, 0] + shift for top in tops]
        layout.append([(0, quarter), (quarter + 16, quarter)])
        targets += [top + site[0, 1] for top in tops]
        layout.append([(j * eighth, eighth) for j in range(4)])
        targets += [top + site[1, 1] + shift for shift in (0, eighth) for top in tops]
    targets = jnp.stack(targets).astype(jnp.int32)

    smem = pl.BlockSpec(memory_space=pltpu.SMEM)
    window_rows = (2 * REACH + 1) * panel
    return pl.pallas_call(
        lambda *refs: purify_kernel(layout, bs, slots, *refs),
        out_shape=jax.ShapeDtypeStruct((row_count, 1, bs, bs), jnp.bfloat16),
        in_specs=[smem] * 4 + [pl.BlockSpec(memory_space=pl.ANY)] * len(pieces),
        out_specs=pl.BlockSpec(memory_space=pltpu.VMEM),
        scratch_shapes=[
            pltpu.VMEM((window_rows + bs, bs), jnp.bfloat16),
            pltpu.SMEM((row_count * 32,), jnp.int32),
            pltpu.SemaphoreType.DMA((sum(map(len, layout)),)),
        ],
        compiler_params=pltpu.CompilerParams(vmem_limit_bytes=10 * 2**20),
        name="purify",
    )(targets, window_cols, wanted, skipped, *pieces)


def solution(mesh):
    placed = (P("blk", None, None, None), P("blk", None), P("blk", "col"))
    return jax.shard_map(
        body, mesh=mesh, in_specs=placed, out_specs=P("blk", "col", None, None), check_vma=False
    )
```

```python
import jax
import jax.numpy as jnp
from jax import lax
from jax.experimental import pallas as pl
from jax.experimental.pallas import tpu as pltpu
from jax.sharding import PartitionSpec as P

REACH = 2
def swap_routes(partner_of):
    return [(partner_of(i), i) for i in range(lax.axis_size("blk"))]


def col_routes(source_of):
    return [(source_of(i) % lax.axis_size("col"), i) for i in range(lax.axis_size("col"))]


def purify_kernel(layout, bs, slots, targets_ref, cols_ref, wanted_ref, skipped_ref, *refs):
    pieces, out_ref, window, picks, sems = refs[:-4], refs[-4], refs[-3], refs[-2], refs[-1]
    row_count = out_ref.shape[0]
    nothing = window.shape[0] // bs - 1
    copies = []
    for ref, moves in zip(pieces, layout, strict=True):
        for source, rows in moves:
            start = pl.multiple_of(targets_ref[len(copies)], bs)
            copies.append(
                pltpu.make_async_copy(
                    ref.at[pl.ds(source, rows)],
                    window.at[pl.ds(start, rows)],
                    sems.at[len(copies)],
                )
            )
            copies[-1].start()
    window[pl.ds(nothing * bs, bs)] = jnp.zeros((bs, window.shape[1]), window.dtype)

    first = REACH * row_count

    def find_row(r, carry):
        column, skipped = wanted_ref[r], skipped_ref[r]
        for a in range(slots):
            base = cols_ref[(first + r) * slots + a] * slots
            for b in range(slots):
                q = cols_ref[base + b]
                found = jnp.int32(nothing)
                for m in range(slots):
                    found = jnp.where(cols_ref[q * slots + m] == column, q * slots + m, found)
                found = jnp.where(q == skipped, nothing, found)
                picks[r * 32 + a * slots + b] = found
                picks[r * 32 + 16 + a * slots + b] = jnp.where(q == column, base + b, nothing)
        return carry

    lax.fori_loop(0, row_count, find_row, 0)
    for copy in copies:
        copy.wait()

    def block(index):
        return window[pl.ds(pl.multiple_of(index * bs, bs), bs)]

    def stack(indices, axis):
        return jnp.concatenate([block(i) for i in indices], axis=axis)

    for r in range(row_count):
        direct, high, low = [], [], []
        for a in range(slots):
            base = cols_ref[(first + r) * slots + a] * slots
            left = stack([base + b for b in range(slots)], 1)
            right = stack([picks[r * 32 + a * slots + b] for b in range(slots)], 0)
            total = jnp.dot(left, right, preferred_element_type=jnp.float32)
            top = total.astype(jnp.bfloat16)
            high.append(top)
            low.append((total - top.astype(jnp.float32)).astype(jnp.bfloat16))
            one = [block(picks[r * 32 + 16 + a * slots + b]) for b in range(slots)]
            direct.append((one[0] + one[1]) + (one[2] + one[3]))
        left = stack([(first + r) * slots + a for a in range(slots)], 1)
        right = jnp.concatenate(
            [jnp.concatenate(part, 0) for part in (direct, high, low)], 1
        )
        sums = jnp.dot(left, right, preferred_element_type=jnp.float32)
        squared = sums[:, :bs].astype(jnp.bfloat16).astype(jnp.float32)
        cubed = sums[:, bs : 2 * bs] + sums[:, 2 * bs :]
        out_ref[r, 0] = (3.0 * squared - 2.0 * cubed).astype(jnp.bfloat16)


def body(pvals, pcols, out_cols):
    row_count, slots, bs, _ = pvals.shape
    panel = row_count * slots * bs
    half, quarter, eighth = panel // 2, panel // 4, panel // 8
    total_rows = row_count * lax.axis_size("blk")
    own = lax.axis_index("blk")
    place = lax.axis_index("col")
    window_start = (own - REACH) * row_count
    parity, core = jnp.bitwise_and(place >> 2, 1), jnp.bitwise_and(place, 1)
    flat = pvals.reshape(panel, bs)
    own_cols = pcols.reshape(-1)
    tail = jnp.zeros((16, bs), jnp.bfloat16)
    tail = tail.at[0, : own_cols.shape[0]].set(own_cols.astype(jnp.bfloat16))

    def parcel(at, rows):
        return jnp.concatenate([lax.dynamic_slice_in_dim(flat, at, rows, 0), tail], 0)

    count = lax.axis_size("blk")
    small = parcel((2 * parity + core) * quarter, quarter)
    late = [
        lax.ppermute(small, "blk", swap_routes(lambda i, d=d: (((i + d) ^ d) - d) % count))
        for d in (1, 2)
    ]
    large = parcel(core * half, half)
    early = [lax.ppermute(large, "blk", swap_routes(lambda i, d=d: i ^ d)) for d in (1, 2)]

    def local(ids):
        return jnp.bitwise_and(ids - window_start, total_rows - 1).astype(jnp.int32)

    wanted = local(out_cols[:, 0])
    bound = REACH * row_count
    rows = jnp.arange(row_count, dtype=jnp.int32)
    offsets = jnp.bitwise_and(wanted - rows, total_rows - 1)
    late, skipped = lax.optimization_barrier((late, lax.psum(offsets, "col")))
    skipped = bound * (2 * bound + 1) - skipped + rows

    def from_core(arrays):
        return lax.ppermute(jnp.concatenate(arrays, 0), "col", col_routes(lambda i: i ^ 1))

    left = lax.ppermute(
        jnp.concatenate([x[:eighth] for x in late], 0), "col", col_routes(lambda i: i - 4)
    )
    right = lax.ppermute(
        jnp.concatenate([x[eighth:quarter] for x in late], 0), "col", col_routes(lambda i: i + 4)
    )
    others = [from_core(early), from_core(late)]
    sides = from_core([left, right])

    def listed(x):
        return x[x.shape[0] - 16, : own_cols.shape[0]]

    odd = [jnp.bitwise_and(own, d) != 0 for d in (1, 2)]
    ahead = [jnp.where(o, listed(x), listed(y)) for o, x, y in zip(odd, late, early)]
    behind = [jnp.where(o, listed(y), listed(x)) for o, x, y in zip(odd, late, early)]
    window_cols = jnp.concatenate(
        [behind[1], behind[0], own_cols.astype(jnp.bfloat16), ahead[0], ahead[1]]
    )
    window_cols = local(window_cols.astype(jnp.int32))
    pieces = [flat, *early, *late, left, right, *others, sides]
    near, far = (
        [(REACH + jnp.where(o, -way, way) * d) * panel for o, d in zip(odd, (1, 2))]
        for way in (1, -1)
    )
    site = {
        (h, c): (2 * (parity ^ h) + (core ^ c)) * quarter for h in (0, 1) for c in (0, 1)
    }
    layout, targets = [[(0, panel)]], [jnp.int32(REACH * panel)]
    layout += [[(0, half)] for _ in near] + [[(0, quarter)] for _ in far]
    targets += [top + core * half for top in near] + [top + site[0, 0] for top in far]
    for shift in (0, eighth):
        layout.append([(0, eighth), (eighth, eighth)])
        targets += [top + site[1, 0] + shift for top in far]
    layout += [[(0, rows), (rows + 16, rows)] for rows in (half, quarter)]
    targets += [top + (1 - core) * half for top in near] + [top + site[0, 1] for top in far]
    layout.append([(j * eighth, eighth) for j in range(4)])
    targets += [top + site[1, 1] + shift for shift in (0, eighth) for top in far]
    targets = jnp.stack(targets).astype(jnp.int32)

    smem = pl.BlockSpec(memory_space=pltpu.SMEM)
    window_rows = (2 * REACH + 1) * panel
    return pl.pallas_call(
        lambda *refs: purify_kernel(layout, bs, slots, *refs),
        out_shape=jax.ShapeDtypeStruct((row_count, 1, bs, bs), jnp.bfloat16),
        in_specs=[smem] * 4 + [pl.BlockSpec(memory_space=pl.ANY)] * len(pieces),
        out_specs=pl.BlockSpec(memory_space=pltpu.VMEM),
        scratch_shapes=[
            pltpu.VMEM((window_rows + bs, bs), jnp.bfloat16),
            pltpu.SMEM((row_count * 32,), jnp.int32),
            pltpu.SemaphoreType.DMA((sum(map(len, layout)),)),
        ],
        compiler_params=pltpu.CompilerParams(vmem_limit_bytes=10 * 2**20),
        name="purify",
    )(targets, window_cols, wanted, skipped, *pieces)


def solution(mesh):
    placed = (P("blk", None, None, None), P("blk", None), P("blk", "col"))
    return jax.shard_map(
        body, mesh=mesh, in_specs=placed, out_specs=P("blk", "col", None, None), check_vma=False
    )
```

```python
import jax
import jax.numpy as jnp
from jax import lax
from jax.experimental import pallas as pl
from jax.experimental.pallas import tpu as pltpu
from jax.sharding import PartitionSpec as P

REACH = 2
def swap_routes(partner_of):
    return [(partner_of(i), i) for i in range(lax.axis_size("blk"))]


def col_routes(source_of):
    return [(source_of(i) % lax.axis_size("col"), i) for i in range(lax.axis_size("col"))]


def purify_kernel(layout, bs, slots, targets_ref, cols_ref, wanted_ref, skipped_ref, *refs):
    pieces, out_ref, window = refs[:-2], refs[-2], refs[-1]
    row_count = out_ref.shape[0]
    nothing = window.shape[0] // bs - 1
    first = REACH * row_count

    moves = [(ref, *move) for ref, given in zip(pieces, layout, strict=True) for move in given]
    for i, (ref, source, rows) in enumerate(moves):
        start = pl.multiple_of(targets_ref[i], bs)
        window[pl.ds(start, rows)] = ref[pl.ds(source, rows)]
    window[pl.ds(nothing * bs, bs)] = jnp.zeros((bs, window.shape[1]), window.dtype)

    def block(index):
        return window[pl.ds(pl.multiple_of(index * bs, bs), bs)]

    def stack(indices, axis):
        return jnp.concatenate([block(i) for i in indices], axis=axis)

    for r in range(row_count):
        column, skipped = wanted_ref[r], skipped_ref[r]
        direct, high, low = [], [], []
        for a in range(slots):
            base = cols_ref[(first + r) * slots + a] * slots
            reached, hit = [], jnp.int32(nothing)
            for b in range(slots):
                q = cols_ref[base + b]
                found = jnp.int32(nothing)
                for m in range(slots):
                    here = q * slots + m
                    found = jnp.where(cols_ref[here] == column, here, found)
                reached.append(jnp.where(q == skipped, nothing, found))
                hit = jnp.where(q == column, base + b, hit)
            total = jnp.dot(
                stack([base + b for b in range(slots)], 1),
                stack(reached, 0),
                preferred_element_type=jnp.float32,
            )
            top = total.astype(jnp.bfloat16)
            high.append(top)
            low.append((total - top.astype(jnp.float32)).astype(jnp.bfloat16))
            direct.append(block(hit))
        left = stack([(first + r) * slots + a for a in range(slots)], 1)
        right = jnp.concatenate(
            [jnp.concatenate(part, 0) for part in (direct, high, low)], 1
        )
        sums = jnp.dot(left, right, preferred_element_type=jnp.float32)
        squared = sums[:, :bs].astype(jnp.bfloat16).astype(jnp.float32)
        cubed = sums[:, bs : 2 * bs] + sums[:, 2 * bs :]
        out_ref[r, 0] = (3.0 * squared - 2.0 * cubed).astype(jnp.bfloat16)


def body(pvals, pcols, out_cols):
    row_count, slots, bs, _ = pvals.shape
    panel = row_count * slots * bs
    half, quarter, eighth = panel // 2, panel // 4, panel // 8
    total_rows = row_count * lax.axis_size("blk")
    own = lax.axis_index("blk")
    place = lax.axis_index("col")
    window_start = (own - REACH) * row_count
    parity, core = jnp.bitwise_and(place >> 2, 1), jnp.bitwise_and(place, 1)
    flat = pvals.reshape(panel, bs)
    own_cols = pcols.reshape(-1)
    tail = jnp.zeros((16, bs), jnp.bfloat16)
    tail = tail.at[0, : own_cols.shape[0]].set(own_cols.astype(jnp.bfloat16))

    def parcel(at, rows):
        return jnp.concatenate([lax.dynamic_slice_in_dim(flat, at, rows, 0), tail], 0)

    count = lax.axis_size("blk")
    small = parcel((2 * parity + core) * quarter, quarter)
    late = [
        lax.ppermute(small, "blk", swap_routes(lambda i, d=d: (((i + d) ^ d) - d) % count))
        for d in (1, 2)
    ]
    large = parcel(core * half, half)
    early = [lax.ppermute(large, "blk", swap_routes(lambda i, d=d: i ^ d)) for d in (1, 2)]

    def local(ids):
        return jnp.bitwise_and(ids - window_start, total_rows - 1).astype(jnp.int32)

    wanted = local(out_cols[:, 0])
    bound = REACH * row_count
    rows = jnp.arange(row_count, dtype=jnp.int32)
    offsets = jnp.bitwise_and(wanted - rows, total_rows - 1)
    late, skipped = lax.optimization_barrier((late, lax.psum(offsets, "col")))
    skipped = bound * (2 * bound + 1) - skipped + rows

    def from_core(arrays):
        return lax.ppermute(jnp.concatenate(arrays, 0), "col", col_routes(lambda i: i ^ 1))

    first = jnp.concatenate([x[:eighth] for x in late], 0)
    second = jnp.concatenate([x[eighth:quarter] for x in late], 0)
    (first, second), early = lax.optimization_barrier(((first, second), early))
    left = lax.ppermute(first, "col", col_routes(lambda i: i - 4))
    right = lax.ppermute(second, "col", col_routes(lambda i: i + 4))
    other = from_core(early)
    sides = from_core([left, right, *late])

    def listed(x):
        return x[x.shape[0] - 16, : own_cols.shape[0]]

    odd = [jnp.bitwise_and(own, d) != 0 for d in (1, 2)]
    ahead = [jnp.where(o, listed(x), listed(y)) for o, x, y in zip(odd, late, early)]
    behind = [jnp.where(o, listed(y), listed(x)) for o, x, y in zip(odd, late, early)]
    window_cols = jnp.concatenate(
        [behind[1], behind[0], own_cols.astype(jnp.bfloat16), ahead[0], ahead[1]]
    )
    window_cols = local(window_cols.astype(jnp.int32))
    pieces = [flat, *early, *late, left, right, other, sides]
    near, far = (
        [(REACH + jnp.where(o, -way, way) * d) * panel for o, d in zip(odd, (1, 2))]
        for way in (1, -1)
    )
    site = {
        (h, c): (2 * (parity ^ h) + (core ^ c)) * quarter for h in (0, 1) for c in (0, 1)
    }
    layout, targets = [[(0, panel)]], [jnp.int32(REACH * panel)]
    layout += [[(0, half)] for _ in near] + [[(0, quarter)] for _ in far]
    targets += [top + core * half for top in near] + [top + site[0, 0] for top in far]
    for shift in (0, eighth):
        layout.append([(0, eighth), (eighth, eighth)])
        targets += [top + site[1, 0] + shift for top in far]
    layout.append([(0, half), (half + 16, half)])
    targets += [top + (1 - core) * half for top in near]
    layout.append([(j * eighth, eighth) for j in range(4)])
    layout[-1] += [(2 * quarter + j * (quarter + 16), quarter) for j in range(2)]
    targets += [top + site[1, 1] + shift for shift in (0, eighth) for top in far]
    targets += [top + site[0, 1] for top in far]
    targets = jnp.stack(targets).astype(jnp.int32)

    smem = pl.BlockSpec(memory_space=pltpu.SMEM)
    window_rows = (2 * REACH + 1) * panel
    return pl.pallas_call(
        lambda *refs: purify_kernel(layout, bs, slots, *refs),
        out_shape=jax.ShapeDtypeStruct((row_count, 1, bs, bs), jnp.bfloat16),
        in_specs=[smem] * 4 + [pl.BlockSpec(memory_space=pltpu.VMEM)] * len(pieces),
        out_specs=pl.BlockSpec(memory_space=pltpu.VMEM),
        scratch_shapes=[
            pltpu.VMEM((window_rows + bs, bs), jnp.bfloat16),
        ],
        compiler_params=pltpu.CompilerParams(vmem_limit_bytes=16 * 2**20),
        name="purify",
    )(targets, window_cols, wanted, skipped, *pieces)


def solution(mesh):
    placed = (P("blk", None, None, None), P("blk", None), P("blk", "col"))
    return jax.shard_map(
        body, mesh=mesh, in_specs=placed, out_specs=P("blk", "col", None, None), check_vma=False
    )
```

```python
import jax
import jax.numpy as jnp
from jax import lax
from jax.experimental import pallas as pl
from jax.experimental.pallas import tpu as pltpu
from jax.sharding import PartitionSpec as P

REACH = 2
def swap_routes(partner_of):
    return [(partner_of(i), i) for i in range(lax.axis_size("blk"))]


def col_routes(source_of):
    return [(source_of(i) % lax.axis_size("col"), i) for i in range(lax.axis_size("col"))]


def purify_kernel(layout, bs, slots, targets_ref, cols_ref, wanted_ref, skipped_ref, *refs):
    pieces, out_ref, window = refs[:-2], refs[-2], refs[-1]
    row_count = out_ref.shape[0]
    nothing = window.shape[0] // bs - 1
    first = REACH * row_count

    moves = [(ref, *move) for ref, given in zip(pieces, layout, strict=True) for move in given]
    for i, (ref, source, rows) in enumerate(moves):
        start = pl.multiple_of(targets_ref[i], bs)
        window[pl.ds(start, rows)] = ref[pl.ds(source, rows)]
    window[pl.ds(nothing * bs, bs)] = jnp.zeros((bs, window.shape[1]), window.dtype)

    def block(index):
        return window[pl.ds(pl.multiple_of(index * bs, bs), bs)]

    def stack(indices, axis):
        return jnp.concatenate([block(i) for i in indices], axis=axis)

    for r in range(row_count):
        column, skipped = wanted_ref[r], skipped_ref[r]
        direct, high, low = [], [], []
        for a in range(slots):
            base = cols_ref[(first + r) * slots + a] * slots
            reached, hit = [], jnp.int32(nothing)
            for b in range(slots):
                q = cols_ref[base + b]
                found = jnp.int32(nothing)
                for m in range(slots):
                    here = q * slots + m
                    found = jnp.where(cols_ref[here] == column, here, found)
                reached.append(jnp.where(q == skipped, nothing, found))
                hit = jnp.where(q == column, base + b, hit)
            total = jnp.dot(
                stack([base + b for b in range(slots)], 1),
                stack(reached, 0),
                preferred_element_type=jnp.float32,
            )
            top = total.astype(jnp.bfloat16)
            high.append(top)
            low.append((total - top.astype(jnp.float32)).astype(jnp.bfloat16))
            direct.append(block(hit))
        left = stack([(first + r) * slots + a for a in range(slots)], 1)
        right = jnp.concatenate(
            [jnp.concatenate(part, 0) for part in (direct, high, low)], 1
        )
        sums = jnp.dot(left, right, preferred_element_type=jnp.float32)
        squared = sums[:, :bs].astype(jnp.bfloat16).astype(jnp.float32)
        cubed = sums[:, bs : 2 * bs] + sums[:, 2 * bs :]
        out_ref[r, 0] = (3.0 * squared - 2.0 * cubed).astype(jnp.bfloat16)


def body(pvals, pcols, out_cols):
    row_count, slots, bs, _ = pvals.shape
    panel = row_count * slots * bs
    half, quarter, eighth = panel // 2, panel // 4, panel // 8
    total_rows = row_count * lax.axis_size("blk")
    own = lax.axis_index("blk")
    place = lax.axis_index("col")
    window_start = (own - REACH) * row_count
    parity, core = jnp.bitwise_and(place >> 2, 1), jnp.bitwise_and(place, 1)
    flat = pvals.reshape(panel, bs)
    own_cols = pcols.reshape(-1)
    tail = jnp.zeros((16, bs), jnp.bfloat16)
    tail = tail.at[0, : own_cols.shape[0]].set(own_cols.astype(jnp.bfloat16))

    def parcel(at, rows):
        return jnp.concatenate([lax.dynamic_slice_in_dim(flat, at, rows, 0), tail], 0)

    count = lax.axis_size("blk")
    small = parcel((2 * parity + core) * quarter, quarter)
    late = [
        lax.ppermute(small, "blk", swap_routes(lambda i, d=d: (((i + d) ^ d) - d) % count))
        for d in (1, 2)
    ]
    large = parcel(core * half, half)
    early = [lax.ppermute(large, "blk", swap_routes(lambda i, d=d: i ^ d)) for d in (1, 2)]

    def local(ids):
        return jnp.bitwise_and(ids - window_start, total_rows - 1).astype(jnp.int32)

    wanted = local(out_cols[:, 0])
    bound = REACH * row_count
    rows = jnp.arange(row_count, dtype=jnp.int32)
    offsets = jnp.bitwise_and(wanted - rows, total_rows - 1)
    late, skipped = lax.optimization_barrier((late, lax.psum(offsets, "col")))
    skipped = bound * (2 * bound + 1) - skipped + rows

    def from_core(arrays):
        return lax.ppermute(jnp.concatenate(arrays, 0), "col", col_routes(lambda i: i ^ 1))

    first = jnp.concatenate([x[:eighth] for x in late], 0)
    second = jnp.concatenate([x[eighth:quarter] for x in late], 0)
    left = lax.ppermute(first, "col", col_routes(lambda i: i - 4))
    right = lax.ppermute(second, "col", col_routes(lambda i: i + 4))
    early = lax.optimization_barrier((early, left, second))[0]
    other = from_core(early)
    right = lax.optimization_barrier((right, early))[0]
    sides = from_core([left, right, *late])

    def listed(x):
        return x[x.shape[0] - 16, : own_cols.shape[0]]

    odd = [jnp.bitwise_and(own, d) != 0 for d in (1, 2)]
    ahead = [jnp.where(o, listed(x), listed(y)) for o, x, y in zip(odd, late, early)]
    behind = [jnp.where(o, listed(y), listed(x)) for o, x, y in zip(odd, late, early)]
    window_cols = jnp.concatenate(
        [behind[1], behind[0], own_cols.astype(jnp.bfloat16), ahead[0], ahead[1]]
    )
    window_cols = local(window_cols.astype(jnp.int32))
    pieces = [flat, *early, *late, left, right, other, sides]
    near, far = (
        [(REACH + jnp.where(o, -way, way) * d) * panel for o, d in zip(odd, (1, 2))]
        for way in (1, -1)
    )
    site = {
        (h, c): (2 * (parity ^ h) + (core ^ c)) * quarter for h in (0, 1) for c in (0, 1)
    }
    layout, targets = [[(0, panel)]], [jnp.int32(REACH * panel)]
    layout += [[(0, half)] for _ in near] + [[(0, quarter)] for _ in far]
    targets += [top + core * half for top in near] + [top + site[0, 0] for top in far]
    for shift in (0, eighth):
        layout.append([(0, eighth), (eighth, eighth)])
        targets += [top + site[1, 0] + shift for top in far]
    layout.append([(0, half), (half + 16, half)])
    targets += [top + (1 - core) * half for top in near]
    layout.append([(j * eighth, eighth) for j in range(4)])
    layout[-1] += [(2 * quarter + j * (quarter + 16), quarter) for j in range(2)]
    targets += [top + site[1, 1] + shift for shift in (0, eighth) for top in far]
    targets += [top + site[0, 1] for top in far]
    targets = jnp.stack(targets).astype(jnp.int32)

    smem = pl.BlockSpec(memory_space=pltpu.SMEM)
    window_rows = (2 * REACH + 1) * panel
    return pl.pallas_call(
        lambda *refs: purify_kernel(layout, bs, slots, *refs),
        out_shape=jax.ShapeDtypeStruct((row_count, 1, bs, bs), jnp.bfloat16),
        in_specs=[smem] * 4 + [pl.BlockSpec(memory_space=pltpu.VMEM)] * len(pieces),
        out_specs=pl.BlockSpec(memory_space=pltpu.VMEM),
        scratch_shapes=[
            pltpu.VMEM((window_rows + bs, bs), jnp.bfloat16),
        ],
        compiler_params=pltpu.CompilerParams(vmem_limit_bytes=16 * 2**20),
        name="purify",
    )(targets, window_cols, wanted, skipped, *pieces)


def solution(mesh):
    placed = (P("blk", None, None, None), P("blk", None), P("blk", "col"))
    return jax.shard_map(
        body, mesh=mesh, in_specs=placed, out_specs=P("blk", "col", None, None), check_vma=False
    )
```

```python
import jax
import jax.numpy as jnp
from jax import lax
from jax.experimental import pallas as pl
from jax.experimental.pallas import tpu as pltpu
from jax.sharding import PartitionSpec as P

REACH = 2
def swap_routes(partner_of):
    return [(partner_of(i), i) for i in range(lax.axis_size("blk"))]


def col_routes(source_of):
    return [(source_of(i) % lax.axis_size("col"), i) for i in range(lax.axis_size("col"))]


def purify_kernel(layout, bs, slots, targets_ref, cols_ref, wanted_ref, skipped_ref, *refs):
    pieces, out_ref, window = refs[:-2], refs[-2], refs[-1]
    row_count = out_ref.shape[0]
    nothing = window.shape[0] // bs - 1
    first = REACH * row_count

    moves = [(ref, *move) for ref, given in zip(pieces, layout, strict=True) for move in given]
    for i, (ref, source, rows) in enumerate(moves):
        start = pl.multiple_of(targets_ref[i], bs)
        window[pl.ds(start, rows)] = ref[pl.ds(source, rows)]
    window[pl.ds(nothing * bs, bs)] = jnp.zeros((bs, window.shape[1]), window.dtype)

    def block(index):
        return window[pl.ds(pl.multiple_of(index * bs, bs), bs)]

    def stack(indices, axis):
        return jnp.concatenate([block(i) for i in indices], axis=axis)

    for r in range(row_count):
        column, skipped = wanted_ref[r], skipped_ref[r]
        direct, high, low = [], [], []
        for a in range(slots):
            base = cols_ref[(first + r) * slots + a] * slots
            reached, hit = [], jnp.int32(nothing)
            for b in range(slots):
                q = cols_ref[base + b]
                found = jnp.int32(nothing)
                for m in range(slots):
                    here = q * slots + m
                    found = jnp.where(cols_ref[here] == column, here, found)
                reached.append(jnp.where(q == skipped, nothing, found))
                hit = jnp.where(q == column, base + b, hit)
            total = jnp.dot(
                stack([base + b for b in range(slots)], 1),
                stack(reached, 0),
                preferred_element_type=jnp.float32,
            )
            top = total.astype(jnp.bfloat16)
            high.append(top)
            low.append((total - top.astype(jnp.float32)).astype(jnp.bfloat16))
            direct.append(block(hit))
        left = stack([(first + r) * slots + a for a in range(slots)], 1)
        right = jnp.concatenate(
            [jnp.concatenate(part, 0) for part in (direct, high, low)], 1
        )
        sums = jnp.dot(left, right, preferred_element_type=jnp.float32)
        squared = sums[:, :bs].astype(jnp.bfloat16).astype(jnp.float32)
        cubed = sums[:, bs : 2 * bs] + sums[:, 2 * bs :]
        out_ref[r, 0] = (3.0 * squared - 2.0 * cubed).astype(jnp.bfloat16)


def body(pvals, pcols, out_cols):
    row_count, slots, bs, _ = pvals.shape
    panel = row_count * slots * bs
    half, quarter, eighth = panel // 2, panel // 4, panel // 8
    total_rows = row_count * lax.axis_size("blk")
    own = lax.axis_index("blk")
    place = lax.axis_index("col")
    window_start = (own - REACH) * row_count
    parity, core = jnp.bitwise_and(place >> 2, 1), jnp.bitwise_and(place, 1)
    flat = pvals.reshape(panel, bs)
    own_cols = pcols.reshape(-1)
    tail = jnp.zeros((16, bs), jnp.bfloat16)
    tail = tail.at[0, : own_cols.shape[0]].set(own_cols.astype(jnp.bfloat16))

    def parcel(at, rows):
        return jnp.concatenate([lax.dynamic_slice_in_dim(flat, at, rows, 0), tail], 0)

    count = lax.axis_size("blk")
    small = parcel((2 * parity + core) * quarter, quarter)
    late = [
        lax.ppermute(small, "blk", swap_routes(lambda i, d=d: (((i + d) ^ d) - d) % count))
        for d in (1, 2)
    ]
    large = parcel(core * half, half)
    early = [lax.ppermute(large, "blk", swap_routes(lambda i, d=d: i ^ d)) for d in (1, 2)]

    def local(ids):
        return jnp.bitwise_and(ids - window_start, total_rows - 1).astype(jnp.int32)

    wanted = local(out_cols[:, 0])
    bound = REACH * row_count
    rows = jnp.arange(row_count, dtype=jnp.int32)
    offsets = jnp.bitwise_and(wanted - rows, total_rows - 1)
    late, skipped = lax.optimization_barrier((late, lax.psum(offsets, "col")))
    skipped = bound * (2 * bound + 1) - skipped + rows

    def from_core(arrays):
        return lax.ppermute(jnp.concatenate(arrays, 0), "col", col_routes(lambda i: i ^ 1))

    left = lax.ppermute(
        jnp.concatenate([x[:eighth] for x in late], 0), "col", col_routes(lambda i: i - 4)
    )
    right = lax.ppermute(
        jnp.concatenate([x[eighth:quarter] for x in late], 0), "col", col_routes(lambda i: i + 4)
    )
    others = [from_core(early), from_core(late)]
    sides = from_core([left, right])

    def listed(x):
        return x[x.shape[0] - 16, : own_cols.shape[0]]

    odd = [jnp.bitwise_and(own, d) != 0 for d in (1, 2)]
    ahead = [jnp.where(o, listed(x), listed(y)) for o, x, y in zip(odd, late, early)]
    behind = [jnp.where(o, listed(y), listed(x)) for o, x, y in zip(odd, late, early)]
    window_cols = jnp.concatenate(
        [behind[1], behind[0], own_cols.astype(jnp.bfloat16), ahead[0], ahead[1]]
    )
    window_cols = local(window_cols.astype(jnp.int32))
    pieces = [flat, *early, *late, left, right, *others, sides]
    near, far = (
        [(REACH + jnp.where(o, -way, way) * d) * panel for o, d in zip(odd, (1, 2))]
        for way in (1, -1)
    )
    site = {
        (h, c): (2 * (parity ^ h) + (core ^ c)) * quarter for h in (0, 1) for c in (0, 1)
    }
    layout, targets = [[(0, panel)]], [jnp.int32(REACH * panel)]
    layout += [[(0, half)] for _ in near] + [[(0, quarter)] for _ in far]
    targets += [top + core * half for top in near] + [top + site[0, 0] for top in far]
    for shift in (0, eighth):
        layout.append([(0, eighth), (eighth, eighth)])
        targets += [top + site[1, 0] + shift for top in far]
    layout += [[(0, rows), (rows + 16, rows)] for rows in (half, quarter)]
    targets += [top + (1 - core) * half for top in near] + [top + site[0, 1] for top in far]
    layout.append([(j * eighth, eighth) for j in range(4)])
    targets += [top + site[1, 1] + shift for shift in (0, eighth) for top in far]
    targets = jnp.stack(targets).astype(jnp.int32)

    smem = pl.BlockSpec(memory_space=pltpu.SMEM)
    window_rows = (2 * REACH + 1) * panel
    return pl.pallas_call(
        lambda *refs: purify_kernel(layout, bs, slots, *refs),
        out_shape=jax.ShapeDtypeStruct((row_count, 1, bs, bs), jnp.bfloat16),
        in_specs=[smem] * 4 + [pl.BlockSpec(memory_space=pltpu.VMEM)] * len(pieces),
        out_specs=pl.BlockSpec(memory_space=pltpu.VMEM),
        scratch_shapes=[
            pltpu.VMEM((window_rows + bs, bs), jnp.bfloat16),
        ],
        compiler_params=pltpu.CompilerParams(vmem_limit_bytes=16 * 2**20),
        name="purify",
    )(targets, window_cols, wanted, skipped, *pieces)


def solution(mesh):
    placed = (P("blk", None, None, None), P("blk", None), P("blk", "col"))
    return jax.shard_map(
        body, mesh=mesh, in_specs=placed, out_specs=P("blk", "col", None, None), check_vma=False
    )
```
